32 devices in a mesh: groups: 2 (over y), row: 4 (over x, core), col: 4 (over z).
Axes of the slice: x: 2, y: 2, z: 4, core: 2. Of those that a mesh axis runs over, the one named last changes fastest.
Arguments:
- tokens: bfloat16 [512, 8192], P(('groups', 'col'), 'row'), parts along dimension 0, may hold values from -6 to 6
- gate_weight: bfloat16 [8192, 14336], P('row', 'col'), may hold values from -0.0625 to 0.0625
- up_weight: bfloat16 [8192, 14336], P('row', 'col'), may hold values from -0.0625 to 0.0625
- down_weight: bfloat16 [14336, 8192], P('col', 'row'), may hold values from -0.046875 to 0.046875
- gate_left: bfloat16 [16384, 512], P(('groups', 'row'), 'col'), parts along dimension 0, may hold values from -0.25 to 0.25
- gate_right: bfloat16 [1024, 14336], P(('groups', 'row'), 'col'), parts along dimension 0, may hold values from -0.0625 to 0.0625
- up_left: bfloat16 [16384, 512], P(('groups', 'row'), 'col'), parts along dimension 0, may hold values from -0.25 to 0.25
- up_right: bfloat16 [1024, 14336], P(('groups', 'row'), 'col'), parts along dimension 0, may hold values from -0.0625 to 0.0625
- down_left: bfloat16 [28672, 512], P(('groups', 'col'), 'row'), parts along dimension 0, may hold values from -0.25 to 0.25
- down_right: bfloat16 [1024, 8192], P(('groups', 'col'), 'row'), parts along dimension 0, may hold values from -0.046875 to 0.046875
Outputs:
- mixed: bfloat16 [512, 8192], P(('groups', 'col'), 'row'), parts along dimension 0
- gate_merged: bfloat16 [16384, 14336], P(('groups', 'row'), 'col'), parts along dimension 0
- up_merged: bfloat16 [16384, 14336], P(('groups', 'row'), 'col'), parts along dimension 0
- down_merged: bfloat16 [28672, 8192], P(('groups', 'col'), 'row'), parts along dimension 0
The draws below stay inside these ranges and needn't reach their ends.
There are 2 independent parts, one for each index of `groups`. The reference program is written for one: setup_inputs(seed, part) draws one part's arguments, and reference() takes and returns one part's arrays. A program takes and returns all parts, laid end to end along the dimension named above; an argument that names none is the same for every part. Nothing has to cross between parts.
All inputs are finite; a program needn't handle non-finite values.
Results may differ from the reference program's by a relative error of at most 0.007.
Values may be sent and summed in bfloat16 or wider, within the bound.
A program may use at most 256 MiB of HBM per device.

```python
import jax
import jax.numpy as jnp

D = 8192
FF = 14336
R = 512
TOKENS = 256


def shard_levels(own_key, dims, shards, smallest, largest):
    def one(dim, parts):
        steps = jax.random.uniform(jax.random.fold_in(jax.random.fold_in(own_key, 6), dim), (parts,), jnp.float32, smallest / len(shards), largest / len(shards))
        return jnp.repeat(jnp.exp(steps), dims[dim] // parts).reshape((-1,) + (1,) * (len(dims) - dim - 1))

    loudness = one(*shards[0])
    for cut in shards[1:]:
        loudness = loudness * one(*cut)
    return loudness


def bell_draw(key, shape, deviation, reach, pieces=(), held_as=jnp.bfloat16):
    result = deviation * jax.random.normal(key, shape, jnp.float32)
    if pieces:
        result = result * shard_levels(key, shape, pieces, -0.22, 0.18)
    return jnp.clip(result, -reach, reach).astype(held_as)


def setup_inputs(seed: int = 0, part: int = 0) -> dict:
    streams_of = jax.random.split(jax.random.key(seed), 11)
    part_splits = jax.random.split(jax.random.fold_in(streams_of[10], part), 11)
    return {
        "tokens": bell_draw(part_splits[0], (TOKENS, D), 1.0, 6.0, ((0, 4), (1, 4))),
        "gate_weight": bell_draw(streams_of[1], (D, FF), D ** -0.5, 0.0625, ((0, 4), (1, 4))),
        "up_weight": bell_draw(streams_of[2], (D, FF), D ** -0.5, 0.0625, ((0, 4), (1, 4))),
        "down_weight": bell_draw(streams_of[3], (FF, D), FF ** -0.5, 0.046875, ((0, 4), (1, 4))),
        "gate_left": bell_draw(part_splits[4], (D, R), R ** -0.5, 0.25, ((0, 4), (1, 4))),
        "gate_right": bell_draw(part_splits[5], (R, FF), D ** -0.5, 0.0625, ((0, 4), (1, 4))),
        "up_left": bell_draw(part_splits[6], (D, R), R ** -0.5, 0.25, ((0, 4), (1, 4))),
        "up_right": bell_draw(part_splits[7], (R, FF), D ** -0.5, 0.0625, ((0, 4), (1, 4))),
        "down_left": bell_draw(part_splits[8], (FF, R), R ** -0.5, 0.25, ((0, 4), (1, 4))),
        "down_right": bell_draw(part_splits[9], (R, D), FF ** -0.5, 0.046875, ((0, 4), (1, 4))),
    }


def merge_delta(weight, left, right):
    delta = jnp.dot(left, right, preferred_element_type=jnp.float32)
    return (weight.astype(jnp.float32) + delta).astype(jnp.bfloat16)


def reference(tokens, gate_weight, up_weight, down_weight, gate_left, gate_right, up_left, up_right, down_left, down_right):
    gate_merged = merge_delta(gate_weight, gate_left, gate_right)
    up_merged = merge_delta(up_weight, up_left, up_right)
    down_merged = merge_delta(down_weight, down_left, down_right)
    gate = jnp.dot(tokens, gate_merged, preferred_element_type=jnp.float32)
    up = jnp.dot(tokens, up_merged, preferred_element_type=jnp.float32)
    hidden = (jax.nn.silu(gate) * up).astype(jnp.bfloat16)
    mixed = jnp.dot(hidden, down_merged, preferred_element_type=jnp.float32)
    return (mixed.astype(jnp.bfloat16), gate_merged, up_merged, down_merged)
```

```python
import functools

import jax
import jax.numpy as jnp
from jax import lax
from jax.experimental import pallas as pl
from jax.experimental.pallas import tpu as pltpu
from jax.sharding import PartitionSpec as P

F32 = jnp.float32
BF16 = jnp.bfloat16


def put(whole, piece, slot, axis):
    start = [0] * whole.ndim
    start[axis] = slot * piece.shape[axis]
    return lax.dynamic_update_slice(whole, piece, start)


def take(whole, slot, size, axis=0):
    return lax.dynamic_slice_in_dim(whole, slot * size, size, axis)


def dot(a, b):
    return jnp.dot(a, b, preferred_element_type=F32)


def merge_delta(weight, left, right):
    return (weight.astype(F32) + dot(left, right)).astype(BF16)


def line_gather(x, axis, n):
    if n != 4:
        return lax.all_gather(x, "col", axis=axis, tiled=True)
    me = lax.axis_index("col")
    ups, downs = [x], [x]
    for step in range(1, n):
        ups.append(lax.ppermute(ups[-1], "col", [(i, i + 1) for i in range(step - 1, n - 1)]))
        downs.append(lax.ppermute(downs[-1], "col", [(i, i - 1) for i in range(1, n - step + 1)]))
    shape = list(x.shape)
    shape[axis] *= n
    whole = put(jnp.zeros(shape, x.dtype), x, me, axis)
    for step in range(1, n):
        piece = jnp.where(me >= step, ups[step], downs[n - step])
        whole = put(whole, piece, lax.rem(me - step + n, n), axis)
    return whole


def row_swap(x, bit):
    return lax.ppermute(x, "row", [(i, i ^ bit) for i in range(4)])


def row_gather(x, axis, n):
    if n != 4:
        return lax.all_gather(x, "row", axis=axis, tiled=True)
    me = lax.axis_index("row")
    far = row_swap(x, 2)
    near = row_swap(x, 1)
    corner = row_swap(far, 1)
    shape = list(x.shape)
    shape[axis] *= n
    whole = jnp.zeros(shape, x.dtype)
    for bit, piece in ((0, x), (1, near), (2, far), (3, corner)):
        whole = put(whole, piece, jnp.bitwise_xor(me, bit), axis)
    return whole


def row_scatter_sum(x, n):
    if n != 4:
        return lax.psum_scatter(x, "row", scatter_dimension=0, tiled=True)
    me = lax.axis_index("row")
    size = x.shape[0] // n
    blocks = x.reshape(2, 2, size, x.shape[1])
    core = me % 2
    kept = lax.dynamic_index_in_dim(blocks, core, 1, keepdims=False)
    given = lax.dynamic_index_in_dim(blocks, 1 - core, 1, keepdims=False)
    both = kept + row_swap(given, 1)
    chip = me // 2
    mine = lax.dynamic_index_in_dim(both, chip, 0, keepdims=False)
    other = lax.dynamic_index_in_dim(both, 1 - chip, 0, keepdims=False)
    return mine + row_swap(other.astype(BF16), 2).astype(F32)


def row_sum(x, n):
    if n != 4:
        return lax.psum(x, "row")
    x = x + row_swap(x, 1)
    return x + row_swap(x, 2)


def turn(x, step, n):
    return lax.ppermute(x, "col", [(i, (i + step) % n) for i in range(n)])


def col_sum(x, n):
    if n != 4:
        return lax.psum(x, "col")
    terms = [turn(x, step, n) for step in range(1, n)]
    for term in terms:
        x = x + term
    return x


def col_scatter_sum(x, n):
    if n != 4:
        return lax.psum_scatter(x, "col", scatter_dimension=0, tiled=True)
    me = lax.axis_index("col")
    size = x.shape[0] // n
    total = take(x, me, size)
    for step in range(1, n):
        block = take(x, lax.rem(me + step, n), size).astype(BF16)
        total = total + turn(block, step, n).astype(F32)
    return total


def gather_kernel(lines, rows, *refs):
    total = len(lines) + len(rows)
    ins, outs = refs[:total], refs[total : 2 * total]
    own_sem, send_sem, recv_sem = refs[2 * total :]
    n = 4
    col, row = lax.axis_index("col"), lax.axis_index("row")
    dims = lines + rows

    barrier = pltpu.get_barrier_semaphore()
    for target in (
        {"col": lax.rem(col + 1, n)},
        {"col": lax.rem(col + n - 1, n)},
        {"row": jnp.bitwise_xor(row, 1)},
        {"row": jnp.bitwise_xor(row, 2)},
    ):
        pl.semaphore_signal(barrier, inc=1, device_id=target, device_id_type=pl.DeviceIdType.MESH)
    pl.semaphore_wait(barrier, 4)

    def view(t, slot):
        size = ins[t].shape[dims[t]]
        part = pl.ds(pl.multiple_of(slot * size, size), size)
        return outs[t].at[part, :] if dims[t] == 0 else outs[t].at[:, part]

    def send(t, slot, first, order, target):
        return pltpu.make_async_remote_copy(
            src_ref=ins[t] if first else view(t, slot),
            dst_ref=view(t, slot),
            send_sem=send_sem.at[t, order],
            recv_sem=recv_sem.at[t, slot],
            device_id=target,
            device_id_type=pl.DeviceIdType.MESH,
        )

    def own(t):
        return pltpu.make_async_copy(ins[t], view(t, col if t < len(lines) else row), own_sem.at[t])

    def relay(t, step, way, act):
        slot, target = col - way * step, col + way
        inside = (slot >= 0) & (slot < n) & (target >= 0) & (target < n)

        @pl.when(inside)
        def _():
            copy = send(t, slot, step == 0, step if way > 0 else 3 + step, {"col": target})
            if act == "wait":
                copy.wait_send()
            else:
                copy.start()

    def arrive(t, step, way):
        slot = col - way * step

        @pl.when((slot >= 0) & (slot < n))
        def _():
            send(t, slot, False, 0, {"col": col}).wait_recv()

    def row_copy(t, order):
        near, far = {"row": jnp.bitwise_xor(row, 1)}, {"row": jnp.bitwise_xor(row, 2)}
        if order == 0:
            return send(t, row, True, 0, far)
        if order == 1:
            return send(t, row, True, 1, near)
        return send(t, jnp.bitwise_xor(row, 2), False, 2, near)

    on_line, on_row = range(len(lines)), range(len(lines), total)
    for t in on_line:
        for way in (1, -1):
            relay(t, 0, way, "start")
    for t in on_row:
        row_copy(t, 0).start()
        row_copy(t, 1).start()
    for t in range(total):
        own(t).start()

    passing = [(t, step) for step in range(1, n) for t in on_line]
    crossing = list(on_row)
    for place, (t, step) in enumerate(passing):
        for way in (1, -1):
            arrive(t, step, way)
            if step < n - 1:
                relay(t, step, way, "start")
        if crossing and place % 2 == 1:
            t = crossing.pop(0)
            send(t, jnp.bitwise_xor(row, 2), False, 0, {"row": row}).wait_recv()
            row_copy(t, 2).start()
    for t in crossing:
        send(t, jnp.bitwise_xor(row, 2), False, 0, {"row": row}).wait_recv()
        row_copy(t, 2).start()
    for t in on_row:
        for bit in (1, 3):
            send(t, jnp.bitwise_xor(row, bit), False, 0, {"row": row}).wait_recv()
        for order in range(3):
            row_copy(t, order).wait_send()
    for t in on_line:
        for way in (1, -1):
            for step in range(n - 1):
                relay(t, step, way, "wait")
    for t in range(total):
        own(t).wait()


def gather_all(nrow, ncol, lines, rows):
    if nrow != 4 or ncol != 4:
        done = [lax.all_gather(x, "col", axis=axis, tiled=True) for x, axis in lines]
        return done + [lax.all_gather(x, "row", axis=axis, tiled=True) for x, axis in rows]
    shapes = []
    for x, axis in lines + rows:
        shape = list(x.shape)
        shape[axis] *= 4
        shapes.append(jax.ShapeDtypeStruct(tuple(shape), x.dtype))
    total = len(shapes)
    moved = sum(s.size * 2 for s in shapes)
    return pl.pallas_call(
        functools.partial(gather_kernel, tuple(a for _, a in lines), tuple(a for _, a in rows)),
        out_shape=shapes,
        in_specs=[pl.BlockSpec(memory_space=pl.ANY)] * total,
        out_specs=[pl.BlockSpec(memory_space=pl.ANY)] * total,
        scratch_shapes=[
            pltpu.SemaphoreType.DMA((total,)),
            pltpu.SemaphoreType.DMA((total, 6)),
            pltpu.SemaphoreType.DMA((total, 4)),
        ],
        compiler_params=pltpu.CompilerParams(collective_id=0, has_side_effects=True),
        cost_estimate=pl.CostEstimate(flops=0, bytes_accessed=moved, transcendentals=0),
    )(*[x for x, _ in lines + rows])


def local(
    nrow,
    ncol,
    tokens,
    gate_weight,
    up_weight,
    down_weight,
    gate_left,
    gate_right,
    up_left,
    up_right,
    down_left,
    down_right,
):
    block, gate_l, up_l, gate_r, up_r, down_l = gather_all(
        nrow,
        ncol,
        [(tokens, 0), (gate_left, 1), (up_left, 1)],
        [(gate_right, 0), (up_right, 0), (down_left, 1)],
    )
    down_right, block = lax.optimization_barrier((down_right, block))
    down_r = lax.all_gather(down_right, "col", axis=0, tiled=True)

    def apply(x, weight, left, right):
        return dot(x, weight) + dot(dot(x, left).astype(BF16), right)

    gate = row_scatter_sum(apply(block, gate_weight, gate_l, gate_r), nrow)
    up = row_scatter_sum(apply(block, up_weight, up_l, up_r), nrow)
    hidden = row_gather((jax.nn.silu(gate) * up).astype(BF16), 0, nrow)
    mixed = col_scatter_sum(apply(hidden, down_weight, down_l, down_r), ncol)

    gate_merged = merge_delta(gate_weight, gate_l, gate_r)
    up_merged = merge_delta(up_weight, up_l, up_r)
    down_merged = merge_delta(down_weight, down_l, down_r)
    return (mixed.astype(BF16), gate_merged, up_merged, down_merged)


def solution(mesh):
    nrow, ncol = mesh.shape["row"], mesh.shape["col"]
    in_specs = (
        P(("groups", "col"), "row"),
        P("row", "col"),
        P("row", "col"),
        P("col", "row"),
        P(("groups", "row"), "col"),
        P(("groups", "row"), "col"),
        P(("groups", "row"), "col"),
        P(("groups", "row"), "col"),
        P(("groups", "col"), "row"),
        P(("groups", "col"), "row"),
    )
    out_specs = (
        P(("groups", "col"), "row"),
        P(("groups", "row"), "col"),
        P(("groups", "row"), "col"),
        P(("groups", "col"), "row"),
    )
    return jax.shard_map(
        lambda *a: local(nrow, ncol, *a), mesh=mesh, in_specs=in_specs, out_specs=out_specs, check_vma=False
    )
```

```python
import functools

import jax
import jax.numpy as jnp
from jax import lax
from jax.experimental import pallas as pl
from jax.experimental.pallas import tpu as pltpu
from jax.sharding import PartitionSpec as P

F32 = jnp.float32
BF16 = jnp.bfloat16


def put(whole, piece, slot, axis):
    start = [0] * whole.ndim
    start[axis] = slot * piece.shape[axis]
    return lax.dynamic_update_slice(whole, piece, start)


def take(whole, slot, size, axis=0):
    return lax.dynamic_slice_in_dim(whole, slot * size, size, axis)


def dot(a, b):
    return jnp.dot(a, b, preferred_element_type=F32)


def merge_delta(weight, left, right):
    return (weight.astype(F32) + dot(left, right)).astype(BF16)


def line_gather(x, axis, n):
    if n != 4:
        return lax.all_gather(x, "col", axis=axis, tiled=True)
    me = lax.axis_index("col")
    ups, downs = [x], [x]
    for step in range(1, n):
        ups.append(lax.ppermute(ups[-1], "col", [(i, i + 1) for i in range(step - 1, n - 1)]))
        downs.append(lax.ppermute(downs[-1], "col", [(i, i - 1) for i in range(1, n - step + 1)]))
    shape = list(x.shape)
    shape[axis] *= n
    whole = put(jnp.zeros(shape, x.dtype), x, me, axis)
    for step in range(1, n):
        piece = jnp.where(me >= step, ups[step], downs[n - step])
        whole = put(whole, piece, lax.rem(me - step + n, n), axis)
    return whole


def row_swap(x, bit):
    return lax.ppermute(x, "row", [(i, i ^ bit) for i in range(4)])


def row_gather(x, axis, n):
    if n != 4:
        return lax.all_gather(x, "row", axis=axis, tiled=True)
    me = lax.axis_index("row")
    far = row_swap(x, 2)
    near = row_swap(x, 1)
    corner = row_swap(far, 1)
    shape = list(x.shape)
    shape[axis] *= n
    whole = jnp.zeros(shape, x.dtype)
    for bit, piece in ((0, x), (1, near), (2, far), (3, corner)):
        whole = put(whole, piece, jnp.bitwise_xor(me, bit), axis)
    return whole


def row_scatter_sum(x, n):
    if n != 4:
        return lax.psum_scatter(x, "row", scatter_dimension=0, tiled=True)
    me = lax.axis_index("row")
    size = x.shape[0] // n
    blocks = x.reshape(2, 2, size, x.shape[1])
    core = me % 2
    kept = lax.dynamic_index_in_dim(blocks, core, 1, keepdims=False)
    given = lax.dynamic_index_in_dim(blocks, 1 - core, 1, keepdims=False)
    both = kept + row_swap(given, 1)
    chip = me // 2
    mine = lax.dynamic_index_in_dim(both, chip, 0, keepdims=False)
    other = lax.dynamic_index_in_dim(both, 1 - chip, 0, keepdims=False)
    return mine + row_swap(other.astype(BF16), 2).astype(F32)


def row_sum(x, n):
    if n != 4:
        return lax.psum(x, "row")
    x = x + row_swap(x, 1)
    return x + row_swap(x, 2)


def turn(x, step, n):
    return lax.ppermute(x, "col", [(i, (i + step) % n) for i in range(n)])


def col_sum(x, n):
    if n != 4:
        return lax.psum(x, "col")
    terms = [turn(x, step, n) for step in range(1, n)]
    for term in terms:
        x = x + term
    return x


def col_scatter_sum(x, n):
    if n != 4:
        return lax.psum_scatter(x, "col", scatter_dimension=0, tiled=True)
    me = lax.axis_index("col")
    size = x.shape[0] // n
    total = take(x, me, size)
    for step in range(1, n):
        block = take(x, lax.rem(me + step, n), size).astype(BF16)
        total = total + turn(block, step, n).astype(F32)
    return total


def gather_kernel(lines, rows, *refs):
    total = len(lines) + len(rows)
    ins, outs = refs[:total], refs[total : 2 * total]
    held, (own_sem, send_sem, recv_sem) = refs[2 * total : 3 * total], refs[3 * total :]
    n = 4
    col, row = lax.axis_index("col"), lax.axis_index("row")
    dims = lines + rows

    barrier = pltpu.get_barrier_semaphore()
    for target in (
        {"col": lax.rem(col + 1, n)},
        {"col": lax.rem(col + n - 1, n)},
        {"row": jnp.bitwise_xor(row, 1)},
        {"row": jnp.bitwise_xor(row, 2)},
    ):
        pl.semaphore_signal(barrier, inc=1, device_id=target, device_id_type=pl.DeviceIdType.MESH)
    pl.semaphore_wait(barrier, 4)

    def view(t, slot):
        size = ins[t].shape[dims[t]]
        part = pl.ds(pl.multiple_of(slot * size, size), size)
        return outs[t].at[part, :] if dims[t] == 0 else outs[t].at[:, part]

    def send(t, slot, first, order, target):
        return pltpu.make_async_remote_copy(
            src_ref=ins[t] if first else view(t, slot),
            dst_ref=view(t, slot),
            send_sem=send_sem.at[t, order],
            recv_sem=recv_sem.at[t, slot],
            device_id=target,
            device_id_type=pl.DeviceIdType.MESH,
        )

    def load(t):
        return pltpu.make_async_copy(ins[t], held[t], own_sem.at[t])

    def store(t):
        return pltpu.make_async_copy(held[t], view(t, col if t < len(lines) else row), own_sem.at[t])

    def relay(t, step, way, act):
        slot, target = col - way * step, col + way
        inside = (slot >= 0) & (slot < n) & (target >= 0) & (target < n)

        @pl.when(inside)
        def _():
            copy = send(t, slot, step == 0, step if way > 0 else 3 + step, {"col": target})
            if act == "wait":
                copy.wait_send()
            else:
                copy.start()

    def arrive(t, step, way):
        slot = col - way * step

        @pl.when((slot >= 0) & (slot < n))
        def _():
            send(t, slot, False, 0, {"col": col}).wait_recv()

    def row_copy(t, order):
        near, far = {"row": jnp.bitwise_xor(row, 1)}, {"row": jnp.bitwise_xor(row, 2)}
        if order == 0:
            return send(t, row, True, 0, far)
        if order == 1:
            return send(t, row, True, 1, near)
        return send(t, jnp.bitwise_xor(row, 2), False, 2, near)

    on_line, on_row = range(len(lines)), range(len(lines), total)
    for t in on_line:
        for way in (1, -1):
            relay(t, 0, way, "start")
    for t in on_row:
        row_copy(t, 0).start()
        row_copy(t, 1).start()
    for t in range(total):
        load(t).start()
    for t in range(total):
        load(t).wait()
        store(t).start()

    passing = [(t, step) for step in range(1, n) for t in on_line]
    crossing = list(on_row)
    for place, (t, step) in enumerate(passing):
        for way in (1, -1):
            arrive(t, step, way)
            if step < n - 1:
                relay(t, step, way, "start")
        if crossing and place % 2 == 1:
            t = crossing.pop(0)
            send(t, jnp.bitwise_xor(row, 2), False, 0, {"row": row}).wait_recv()
            row_copy(t, 2).start()
    for t in crossing:
        send(t, jnp.bitwise_xor(row, 2), False, 0, {"row": row}).wait_recv()
        row_copy(t, 2).start()
    for t in on_row:
        for bit in (1, 3):
            send(t, jnp.bitwise_xor(row, bit), False, 0, {"row": row}).wait_recv()
        for order in range(3):
            row_copy(t, order).wait_send()
    for t in on_line:
        for way in (1, -1):
            for step in range(n - 1):
                relay(t, step, way, "wait")
    for t in range(total):
        store(t).wait()


def gather_all(nrow, ncol, lines, rows):
    if nrow != 4 or ncol != 4:
        done = [lax.all_gather(x, "col", axis=axis, tiled=True) for x, axis in lines]
        return done + [lax.all_gather(x, "row", axis=axis, tiled=True) for x, axis in rows]
    shapes = []
    for x, axis in lines + rows:
        shape = list(x.shape)
        shape[axis] *= 4
        shapes.append(jax.ShapeDtypeStruct(tuple(shape), x.dtype))
    total = len(shapes)
    moved = sum(s.size * 2 for s in shapes)
    return pl.pallas_call(
        functools.partial(gather_kernel, tuple(a for _, a in lines), tuple(a for _, a in rows)),
        out_shape=shapes,
        in_specs=[pl.BlockSpec(memory_space=pl.ANY)] * total,
        out_specs=[pl.BlockSpec(memory_space=pl.ANY)] * total,
        scratch_shapes=[pltpu.VMEM(x.shape, x.dtype) for x, _ in lines + rows]
        + [
            pltpu.SemaphoreType.DMA((total,)),
            pltpu.SemaphoreType.DMA((total, 6)),
            pltpu.SemaphoreType.DMA((total, 4)),
        ],
        compiler_params=pltpu.CompilerParams(collective_id=0, has_side_effects=True, vmem_limit_bytes=60 << 20),
        cost_estimate=pl.CostEstimate(flops=0, bytes_accessed=moved, transcendentals=0),
    )(*[x for x, _ in lines + rows])


def merge_apply_kernel(step, x_ref, weight_ref, left_ref, right_ref, merged_ref, out_ref):
    total = None
    for start in range(0, weight_ref.shape[0], step):
        rows = pl.ds(start, step)
        delta = dot(left_ref[rows, :], right_ref[...])
        merged = (weight_ref[rows, :].astype(F32) + delta).astype(BF16)
        merged_ref[rows, :] = merged
        term = dot(x_ref[:, rows], merged)
        total = term if total is None else total + term
    out_ref[...] = total


def merge_apply(x, weight, left, right):
    depth, width = weight.shape
    tile = 512 if width % 512 == 0 else 128
    step = 512 if depth % 512 == 0 else depth
    ranks = left.shape[1]
    return pl.pallas_call(
        functools.partial(merge_apply_kernel, step),
        grid=(width // tile,),
        in_specs=[
            pl.BlockSpec(x.shape, lambda j: (0, 0)),
            pl.BlockSpec((depth, tile), lambda j: (0, j)),
            pl.BlockSpec((depth, ranks), lambda j: (0, 0)),
            pl.BlockSpec((ranks, tile), lambda j: (0, j)),
        ],
        out_specs=[
            pl.BlockSpec((depth, tile), lambda j: (0, j)),
            pl.BlockSpec((x.shape[0], tile), lambda j: (0, j)),
        ],
        out_shape=[
            jax.ShapeDtypeStruct(weight.shape, BF16),
            jax.ShapeDtypeStruct((x.shape[0], width), F32),
        ],
        compiler_params=pltpu.CompilerParams(vmem_limit_bytes=60 << 20),
        cost_estimate=pl.CostEstimate(
            flops=2 * depth * width,
            bytes_accessed=width,
            transcendentals=0,
        ),
    )(x, weight, left, right)


def local(
    nrow,
    ncol,
    tokens,
    gate_weight,
    up_weight,
    down_weight,
    gate_left,
    gate_right,
    up_left,
    up_right,
    down_left,
    down_right,
):
    block, gate_l, up_l, gate_r, up_r, down_l = gather_all(
        nrow,
        ncol,
        [(tokens, 0), (gate_left, 1), (up_left, 1)],
        [(gate_right, 0), (up_right, 0), (down_left, 1)],
    )
    down_right, block = lax.optimization_barrier((down_right, block))
    down_r = lax.all_gather(down_right, "col", axis=0, tiled=True)

    gate_merged, gate_terms = merge_apply(block, gate_weight, gate_l, gate_r)
    gate = row_scatter_sum(gate_terms, nrow)
    up_merged, up_terms = merge_apply(block, up_weight, up_l, up_r)
    up = row_scatter_sum(up_terms, nrow)
    down_merged = merge_delta(down_weight, down_l, down_r)
    hidden = row_gather((jax.nn.silu(gate) * up).astype(BF16), 0, nrow)
    mixed = col_scatter_sum(dot(hidden, down_merged), ncol)
    return (mixed.astype(BF16), gate_merged, up_merged, down_merged)


def solution(mesh):
    nrow, ncol = mesh.shape["row"], mesh.shape["col"]
    in_specs = (
        P(("groups", "col"), "row"),
        P("row", "col"),
        P("row", "col"),
        P("col", "row"),
        P(("groups", "row"), "col"),
        P(("groups", "row"), "col"),
        P(("groups", "row"), "col"),
        P(("groups", "row"), "col"),
        P(("groups", "col"), "row"),
        P(("groups", "col"), "row"),
    )
    out_specs = (
        P(("groups", "col"), "row"),
        P(("groups", "row"), "col"),
        P(("groups", "row"), "col"),
        P(("groups", "col"), "row"),
    )
    return jax.shard_map(
        lambda *a: local(nrow, ncol, *a), mesh=mesh, in_specs=in_specs, out_specs=out_specs, check_vma=False
    )
```

```python
import functools

import jax
import jax.numpy as jnp
from jax import lax
from jax.experimental import pallas as pl
from jax.experimental.pallas import tpu as pltpu
from jax.sharding import PartitionSpec as P

F32 = jnp.float32
BF16 = jnp.bfloat16


def put(whole, piece, slot, axis):
    start = [0] * whole.ndim
    start[axis] = slot * piece.shape[axis]
    return lax.dynamic_update_slice(whole, piece, start)


def take(whole, slot, size, axis=0):
    return lax.dynamic_slice_in_dim(whole, slot * size, size, axis)


def dot(a, b):
    return jnp.dot(a, b, preferred_element_type=F32)


def line_gather(x, axis, n):
    if n != 4:
        return lax.all_gather(x, "col", axis=axis, tiled=True)
    me = lax.axis_index("col")
    ups, downs = [x], [x]
    for step in range(1, n):
        ups.append(lax.ppermute(ups[-1], "col", [(i, i + 1) for i in range(step - 1, n - 1)]))
        downs.append(lax.ppermute(downs[-1], "col", [(i, i - 1) for i in range(1, n - step + 1)]))
    shape = list(x.shape)
    shape[axis] *= n
    whole = put(jnp.zeros(shape, x.dtype), x, me, axis)
    for step in range(1, n):
        piece = jnp.where(me >= step, ups[step], downs[n - step])
        whole = put(whole, piece, lax.rem(me - step + n, n), axis)
    return whole


def row_swap(x, bit):
    return lax.ppermute(x, "row", [(i, i ^ bit) for i in range(4)])


def row_gather(x, axis, n):
    if n != 4:
        return lax.all_gather(x, "row", axis=axis, tiled=True)
    me = lax.axis_index("row")
    far = row_swap(x, 2)
    near = row_swap(x, 1)
    corner = row_swap(far, 1)
    shape = list(x.shape)
    shape[axis] *= n
    whole = jnp.zeros(shape, x.dtype)
    for bit, piece in ((0, x), (1, near), (2, far), (3, corner)):
        whole = put(whole, piece, jnp.bitwise_xor(me, bit), axis)
    return whole


def row_scatter_sum(x, n):
    if n != 4:
        return lax.psum_scatter(x, "row", scatter_dimension=0, tiled=True)
    me = lax.axis_index("row")
    size = x.shape[0] // n
    blocks = x.reshape(2, 2, size, x.shape[1])
    core = me % 2
    kept = lax.dynamic_index_in_dim(blocks, core, 1, keepdims=False)
    given = lax.dynamic_index_in_dim(blocks, 1 - core, 1, keepdims=False)
    both = kept + row_swap(given, 1)
    chip = me // 2
    mine = lax.dynamic_index_in_dim(both, chip, 0, keepdims=False)
    other = lax.dynamic_index_in_dim(both, 1 - chip, 0, keepdims=False)
    return mine + row_swap(other.astype(BF16), 2).astype(F32)


def row_sum(x, n):
    if n != 4:
        return lax.psum(x, "row")
    x = x + row_swap(x, 1)
    return x + row_swap(x, 2)


def turn(x, step, n):
    return lax.ppermute(x, "col", [(i, (i + step) % n) for i in range(n)])


def col_sum(x, n):
    if n != 4:
        return lax.psum(x, "col")
    terms = [turn(x, step, n) for step in range(1, n)]
    for term in terms:
        x = x + term
    return x


def col_scatter_sum(x, n):
    if n != 4:
        return lax.psum_scatter(x, "col", scatter_dimension=0, tiled=True)
    me = lax.axis_index("col")
    size = x.shape[0] // n
    total = take(x, me, size)
    for step in range(1, n):
        block = take(x, lax.rem(me + step, n), size).astype(BF16)
        total = total + turn(block, step, n).astype(F32)
    return total


def gather_kernel(lines, rows, *refs):
    total = len(lines) + len(rows)
    ins, outs = refs[:total], refs[total : 2 * total]
    held, (own_sem, send_sem, recv_sem) = refs[2 * total : 3 * total], refs[3 * total :]
    n = 4
    col, row = lax.axis_index("col"), lax.axis_index("row")
    dims = lines + rows

    barrier = pltpu.get_barrier_semaphore()
    for target in (
        {"col": lax.rem(col + 1, n)},
        {"col": lax.rem(col + n - 1, n)},
        {"row": jnp.bitwise_xor(row, 1)},
        {"row": jnp.bitwise_xor(row, 2)},
    ):
        pl.semaphore_signal(barrier, inc=1, device_id=target, device_id_type=pl.DeviceIdType.MESH)
    pl.semaphore_wait(barrier, 4)

    def view(t, slot):
        size = ins[t].shape[dims[t]]
        part = pl.ds(pl.multiple_of(slot * size, size), size)
        return outs[t].at[part, :] if dims[t] == 0 else outs[t].at[:, part]

    def send(t, slot, first, order, target):
        return pltpu.make_async_remote_copy(
            src_ref=ins[t] if first else view(t, slot),
            dst_ref=view(t, slot),
            send_sem=send_sem.at[t, order],
            recv_sem=recv_sem.at[t, slot],
            device_id=target,
            device_id_type=pl.DeviceIdType.MESH,
        )

    def load(t):
        return pltpu.make_async_copy(ins[t], held[t], own_sem.at[t])

    def store(t):
        return pltpu.make_async_copy(held[t], view(t, col if t < len(lines) else row), own_sem.at[t])

    def relay(t, step, way, act):
        slot, target = col - way * step, col + way
        inside = (slot >= 0) & (slot < n) & (target >= 0) & (target < n)

        @pl.when(inside)
        def _():
            copy = send(t, slot, step == 0, step if way > 0 else 3 + step, {"col": target})
            if act == "wait":
                copy.wait_send()
            else:
                copy.start()

    def arrive(t, step, way):
        slot = col - way * step

        @pl.when((slot >= 0) & (slot < n))
        def _():
            send(t, slot, False, 0, {"col": col}).wait_recv()

    def row_copy(t, order):
        near, far = {"row": jnp.bitwise_xor(row, 1)}, {"row": jnp.bitwise_xor(row, 2)}
        if order == 0:
            return send(t, row, True, 0, far)
        if order == 1:
            return send(t, row, True, 1, near)
        return send(t, jnp.bitwise_xor(row, 2), False, 2, near)

    on_line, on_row = range(len(lines)), range(len(lines), total)
    for t in on_line:
        for way in (1, -1):
            relay(t, 0, way, "start")
    for t in on_row:
        row_copy(t, 0).start()
        row_copy(t, 1).start()
    for t in range(total):
        load(t).start()
    for t in range(total):
        load(t).wait()
        store(t).start()

    passing = [(t, step) for step in range(1, n) for t in on_line]
    crossing = list(on_row)
    for place, (t, step) in enumerate(passing):
        for way in (1, -1):
            arrive(t, step, way)
            if step < n - 1:
                relay(t, step, way, "start")
        if crossing and place % 2 == 1:
            t = crossing.pop(0)
            send(t, jnp.bitwise_xor(row, 2), False, 0, {"row": row}).wait_recv()
            row_copy(t, 2).start()
    for t in crossing:
        send(t, jnp.bitwise_xor(row, 2), False, 0, {"row": row}).wait_recv()
        row_copy(t, 2).start()
    for t in on_row:
        for bit in (1, 3):
            send(t, jnp.bitwise_xor(row, bit), False, 0, {"row": row}).wait_recv()
        for order in range(3):
            row_copy(t, order).wait_send()
    for t in on_line:
        for way in (1, -1):
            for step in range(n - 1):
                relay(t, step, way, "wait")
    for t in range(total):
        store(t).wait()


def gather_all(nrow, ncol, lines, rows):
    if nrow != 4 or ncol != 4:
        done = [lax.all_gather(x, "col", axis=axis, tiled=True) for x, axis in lines]
        return done + [lax.all_gather(x, "row", axis=axis, tiled=True) for x, axis in rows]
    shapes = []
    for x, axis in lines + rows:
        shape = list(x.shape)
        shape[axis] *= 4
        shapes.append(jax.ShapeDtypeStruct(tuple(shape), x.dtype))
    total = len(shapes)
    moved = sum(s.size * 2 for s in shapes)
    return pl.pallas_call(
        functools.partial(gather_kernel, tuple(a for _, a in lines), tuple(a for _, a in rows)),
        out_shape=shapes,
        in_specs=[pl.BlockSpec(memory_space=pl.ANY)] * total,
        out_specs=[pl.BlockSpec(memory_space=pl.ANY)] * total,
        scratch_shapes=[pltpu.VMEM(x.shape, x.dtype) for x, _ in lines + rows]
        + [
            pltpu.SemaphoreType.DMA((total,)),
            pltpu.SemaphoreType.DMA((total, 6)),
            pltpu.SemaphoreType.DMA((total, 4)),
        ],
        compiler_params=pltpu.CompilerParams(collective_id=0, has_side_effects=True, vmem_limit_bytes=60 << 20),
        cost_estimate=pl.CostEstimate(flops=0, bytes_accessed=moved, transcendentals=0),
    )(*[x for x, _ in lines + rows])


def merge_apply_kernel(step, x_ref, weight_ref, left_ref, right_ref, merged_ref, out_ref):
    total = None
    for start in range(0, weight_ref.shape[0], step):
        rows = pl.ds(start, step)
        delta = dot(left_ref[rows, :], right_ref[...])
        merged = (weight_ref[rows, :].astype(F32) + delta).astype(BF16)
        merged_ref[rows, :] = merged
        term = dot(x_ref[:, rows], merged)
        total = term if total is None else total + term
    out_ref[...] = total


def merge_apply(x, weight, left, right):
    depth, width = weight.shape
    tile = 512 if width % 512 == 0 else 128
    step = 512 if depth % 512 == 0 else depth
    ranks = left.shape[1]
    return pl.pallas_call(
        functools.partial(merge_apply_kernel, step),
        grid=(width // tile,),
        in_specs=[
            pl.BlockSpec(x.shape, lambda j: (0, 0)),
            pl.BlockSpec((depth, tile), lambda j: (0, j)),
            pl.BlockSpec((depth, ranks), lambda j: (0, 0)),
            pl.BlockSpec((ranks, tile), lambda j: (0, j)),
        ],
        out_specs=[
            pl.BlockSpec((depth, tile), lambda j: (0, j)),
            pl.BlockSpec((x.shape[0], tile), lambda j: (0, j)),
        ],
        out_shape=[
            jax.ShapeDtypeStruct(weight.shape, BF16),
            jax.ShapeDtypeStruct((x.shape[0], width), F32),
        ],
        compiler_params=pltpu.CompilerParams(vmem_limit_bytes=60 << 20),
        cost_estimate=pl.CostEstimate(
            flops=2 * depth * width,
            bytes_accessed=width,
            transcendentals=0,
        ),
    )(x, weight, left, right)


def local(
    nrow,
    ncol,
    tokens,
    gate_weight,
    up_weight,
    down_weight,
    gate_left,
    gate_right,
    up_left,
    up_right,
    down_left,
    down_right,
):
    block, gate_l, up_l, gate_r, up_r, down_l = gather_all(
        nrow,
        ncol,
        [(tokens, 0), (gate_left, 1), (up_left, 1)],
        [(gate_right, 0), (up_right, 0), (down_left, 1)],
    )
    down_right, block = lax.optimization_barrier((down_right, block))
    down_r = lax.all_gather(down_right, "col", axis=0, tiled=True)

    gate_merged, gate_terms = merge_apply(block, gate_weight, gate_l, gate_r)
    gate = row_scatter_sum(gate_terms, nrow)
    up_merged, up_terms = merge_apply(block, up_weight, up_l, up_r)
    up = row_scatter_sum(up_terms, nrow)
    hidden = row_gather((jax.nn.silu(gate) * up).astype(BF16), 0, nrow)
    down_merged, down_terms = merge_apply(hidden, down_weight, down_l, down_r)
    mixed = col_scatter_sum(down_terms, ncol)
    return (mixed.astype(BF16), gate_merged, up_merged, down_merged)


def solution(mesh):
    nrow, ncol = mesh.shape["row"], mesh.shape["col"]
    in_specs = (
        P(("groups", "col"), "row"),
        P("row", "col"),
        P("row", "col"),
        P("col", "row"),
        P(("groups", "row"), "col"),
        P(("groups", "row"), "col"),
        P(("groups", "row"), "col"),
        P(("groups", "row"), "col"),
        P(("groups", "col"), "row"),
        P(("groups", "col"), "row"),
    )
    out_specs = (
        P(("groups", "col"), "row"),
        P(("groups", "row"), "col"),
        P(("groups", "row"), "col"),
        P(("groups", "col"), "row"),
    )
    return jax.shard_map(
        lambda *a: local(nrow, ncol, *a), mesh=mesh, in_specs=in_specs, out_specs=out_specs, check_vma=False
    )
```
